32 devices in a mesh: wide: 4 (over z), narrow: 8 (over y, x, core).
Axes of the slice: x: 2, y: 2, z: 4, core: 2. Of those that a mesh axis runs over, the one named last changes fastest.
Arguments:
- hidden_in: float32 [2, 32, 8192], P(None, None, 'narrow'), may hold values from -100 to 100
- attn_gain: float32 [8192], P('narrow'), may hold values from 0.1 to 1.9
- w_query: bfloat16 [8192, 8192], P('narrow', 'wide'), may hold values from -0.0625 to 0.0625
- w_key: bfloat16 [8192, 1024], P('narrow', 'wide'), may hold values from -0.0625 to 0.0625
- w_value: bfloat16 [8192, 1024], P('narrow', 'wide'), may hold values from -0.0625 to 0.0625
- w_out: bfloat16 [8192, 8192], P('wide', 'narrow'), may hold values from -0.0625 to 0.0625
- ffn_gain: float32 [8192], P('narrow'), may hold values from 0.1 to 1.9
- w_gate: bfloat16 [8192, 28672], P('narrow', 'wide'), may hold values from -0.0625 to 0.0625
- w_up: bfloat16 [8192, 28672], P('narrow', 'wide'), may hold values from -0.0625 to 0.0625
- w_down: bfloat16 [28672, 8192], P('wide', 'narrow'), may hold values from -0.03125 to 0.03125
- key_cache: bfloat16 [2, 32, 8, 2048, 128], P(None, 'narrow', 'wide'), may hold values from -256 to 256
- value_cache: bfloat16 [2, 32, 8, 2048, 128], P(None, 'narrow', 'wide'), may hold values from -6 to 6
- cache_len: int32 [2, 32], P(None, 'narrow'), may hold values from 1 to 2048, as said below
Outputs:
- hidden_out: float32 [2, 32, 8192], P(None, None, 'narrow')
The draws below stay inside these ranges and needn't reach their ends.
Inputs may be any that keep to these rules, and one draw needn't show every extreme that they name: `cache_len`: in every micro-batch one row's cache holds exactly 2048 tokens.
All inputs are finite; a program needn't handle non-finite values.
Results may differ from the reference program's by a relative error of at most 0.0086.
Values may be sent and summed in bfloat16 or wider, within the bound.
A program may use at most 128 MiB of HBM per device.

```python
import math
import jax
import jax.numpy as jnp
from jax import lax

D = 8192
FF = 28672
QH = 64
KV = 8
HD = 128
MB = 2
CACHE = 2048
ROWS = 32


def draw_hidden_in(key, part):
    key = jax.random.fold_in(key, 1)
    first_key, second_key, third_key = jax.random.split(key, 3)
    base = jnp.clip(jax.random.normal(first_key, (MB, ROWS, D), jnp.float32), -6.0, 6.0)
    row_scale = jnp.exp(jax.random.uniform(second_key, (MB, ROWS, 1), jnp.float32, math.log(0.3), math.log(3.0)))
    column_scale = jnp.exp(jax.random.uniform(third_key, (1, 1, D), jnp.float32, math.log(0.4), math.log(2.5)))
    trend = 3.0 ** (jnp.arange(D, dtype=jnp.float32) / D - 0.5)
    return base * row_scale * column_scale * trend[None, None, :]


def draw_key_cache(key, part):
    key = jax.random.fold_in(key, 3)
    first_key = jax.random.fold_in(key, 0)
    shape = (MB, ROWS, KV, CACHE, HD)
    base = jnp.clip(jax.random.normal(first_key, shape, jnp.float32), -6.0, 6.0)
    return base.astype(jnp.bfloat16)


def draw_cache_len(key, part):
    key = jax.random.fold_in(key, 2)
    first_key, second_key, third_key = jax.random.split(key, 3)
    left = jax.random.randint(first_key, (MB, ROWS), 0, CACHE)
    right = jax.random.randint(second_key, (MB, ROWS), 0, CACHE)
    lengths = 1 + left * right // CACHE
    chosen = jax.random.randint(third_key, (MB, 1), 0, ROWS)
    lengths = jnp.where(jnp.arange(ROWS)[None, :] == chosen, CACHE, lengths)
    return lengths.astype(jnp.int32)


def block_levels(own_key, dims, cuts, low, top_value):
    def one(axis_at, shards_of):
        heights = jax.random.uniform(jax.random.fold_in(jax.random.fold_in(own_key, 6), axis_at), (shards_of,), jnp.float32, low / len(cuts), top_value / len(cuts))
        return jnp.repeat(jnp.exp(heights), dims[axis_at] // shards_of).reshape((-1,) + (1,) * (len(dims) - axis_at - 1))

    gain = one(*cuts[0])
    for cut in cuts[1:]:
        gain = gain * one(*cut)
    return gain


def noise(stream_key, shape, deviation, reach, pieces=(), kind=jnp.bfloat16):
    result = jax.random.normal(stream_key, shape, jnp.float32) * deviation
    if len(pieces) > 0:
        result = block_levels(stream_key, shape, pieces, -0.22, 0.18) * result
    return jnp.clip(result, min=-reach, max=reach).astype(kind)


def setup_inputs(seed: int = 0) -> dict:
    splits = jax.random.split(jax.random.key(seed), 14)
    hidden_in = draw_hidden_in(jax.random.fold_in(splits[13], 71), 0)
    attn_gain = jnp.clip(1.0 + 0.18 * jax.random.normal(splits[1], (D,), jnp.float32), 0.1, 1.9)
    w_query = noise(splits[2], (D, QH * HD), D ** -0.5, 0.0625, ((0, 8), (1, 4)))
    w_key = noise(splits[3], (D, KV * HD), D ** -0.5, 0.0625, ((0, 8), (1, 4)))
    w_value = noise(splits[4], (D, KV * HD), D ** -0.5, 0.0625, ((0, 8), (1, 4)))
    w_out = noise(splits[5], (QH * HD, D), (QH * HD) ** -0.5, 0.0625, ((0, 4), (1, 8)))
    ffn_gain = jnp.clip(1.0 + 0.18 * jax.random.normal(splits[6], (D,), jnp.float32), 0.1, 1.9)
    w_gate = noise(splits[7], (D, FF), D ** -0.5, 0.0625, ((0, 8), (1, 4)))
    w_up = noise(splits[8], (D, FF), D ** -0.5, 0.0625, ((0, 8), (1, 4)))
    w_down = noise(splits[9], (FF, D), FF ** -0.5, 0.03125, ((0, 4), (1, 8)))
    key_cache = draw_key_cache(jax.random.fold_in(splits[13], 71), 0)
    value_cache = noise(splits[11], (MB, ROWS, KV, CACHE, HD), 1.0, 6.0, ((1, 8), (2, 4)))
    cache_len = draw_cache_len(jax.random.fold_in(splits[13], 71), 0)
    return dict(hidden_in=hidden_in, attn_gain=attn_gain, w_query=w_query, w_key=w_key, w_value=w_value, w_out=w_out, ffn_gain=ffn_gain, w_gate=w_gate, w_up=w_up, w_down=w_down, key_cache=key_cache, value_cache=value_cache, cache_len=cache_len)


epsilon = 1e-05

def rotate(values, places):
    halfway = values.shape[-1] // 2
    angles_base = 500000.0 ** (-jnp.arange(halfway, dtype=jnp.float32) * 2.0 / values.shape[-1])
    angles = places * angles_base
    cosines = jnp.cos(angles)
    sinewave = jnp.sin(angles)
    lower_half = values[..., :halfway]
    upper_half = values[..., halfway:]
    return jnp.concatenate([lower_half * cosines - upper_half * sinewave, upper_half * cosines + lower_half * sinewave], axis=-1)

def attend(queries, key_new, value_new, key_rows, value_rows, length):
    scaling = queries.shape[-1] ** (-0.5)
    scores = jnp.einsum('kgd,kld->kgl', queries.astype(jnp.float32), key_rows.astype(jnp.float32)) * scaling
    visible = jnp.arange(key_rows.shape[1]) < length
    scores = jnp.where(visible, scores, -jnp.inf)
    own_score = jnp.einsum('kgd,kd->kg', queries.astype(jnp.float32), key_new.astype(jnp.float32)) * scaling
    highest = jnp.maximum(lax.optimization_barrier(jnp.max(scores, axis=-1)), own_score)
    shifted = jnp.exp(scores - highest[..., None])
    own_term = jnp.exp(own_score - highest)
    totals = lax.optimization_barrier(jnp.sum(shifted, axis=-1)) + own_term
    weights = (shifted / totals[..., None]).astype(jnp.bfloat16)
    own_weight = (own_term / totals).astype(jnp.bfloat16)
    attended = jnp.einsum('kgl,kld->kgd', weights.astype(jnp.float32), value_rows.astype(jnp.float32))
    attended = attended + own_weight.astype(jnp.float32)[..., None] * value_new.astype(jnp.float32)[:, None, :]
    return attended.astype(jnp.bfloat16)

def reference(hidden_in, attn_gain, w_query, w_key, w_value, w_out, ffn_gain, w_gate, w_up, w_down, key_cache, value_cache, cache_len):
    results = []
    for micro_index in range(MB):
        stream = hidden_in[micro_index]
        factor = lax.rsqrt(lax.optimization_barrier(jnp.sum(stream * stream, axis=-1)) / D + epsilon)[:, None]
        normed = (stream * attn_gain).astype(jnp.bfloat16)
        query_sum = jnp.dot(normed, w_query, preferred_element_type=jnp.float32) * factor
        key_sum = jnp.dot(normed, w_key, preferred_element_type=jnp.float32) * factor
        value_sum = jnp.dot(normed, w_value, preferred_element_type=jnp.float32) * factor
        places = cache_len[micro_index].astype(jnp.float32)[:, None, None]
        queries = rotate(query_sum.reshape(ROWS, QH, HD), places).astype(jnp.bfloat16)
        keys_new = rotate(key_sum.reshape(ROWS, KV, HD), places).astype(jnp.bfloat16)
        values_new = value_sum.reshape(ROWS, KV, HD).astype(jnp.bfloat16)
        queries = queries.reshape(ROWS, KV, QH // KV, HD)

        def one_row(packed):
            return attend(*packed)
        attended = lax.map(one_row, (queries, keys_new, values_new, key_cache[micro_index], value_cache[micro_index], cache_len[micro_index]))
        attended = attended.reshape(ROWS, QH * HD)
        middle = stream + jnp.dot(attended, w_out, preferred_element_type=jnp.float32)
        factor_two = lax.rsqrt(lax.optimization_barrier(jnp.sum(middle * middle, axis=-1)) / D + epsilon)[:, None]
        normed_two = (middle * ffn_gain).astype(jnp.bfloat16)
        gate_sum = jnp.dot(normed_two, w_gate, preferred_element_type=jnp.float32) * factor_two
        up_sum = jnp.dot(normed_two, w_up, preferred_element_type=jnp.float32) * factor_two
        hidden = (jax.nn.silu(gate_sum) * up_sum).astype(jnp.bfloat16)
        results.append(middle + jnp.dot(hidden, w_down, preferred_element_type=jnp.float32))
    return jnp.stack(results)
```

```python
import functools

import jax
import jax.numpy as jnp
from jax import lax
from jax.experimental import pallas as pl
from jax.experimental.pallas import tpu as pltpu
from jax.sharding import PartitionSpec as P

D = 8192


epsilon = 1e-05
MESH = pl.DeviceIdType.MESH


def rotate(values, places):
    halfway = values.shape[-1] // 2
    angles_base = 500000.0 ** (-jnp.arange(halfway, dtype=jnp.float32) * 2.0 / values.shape[-1])
    angles = places * angles_base
    cosines = jnp.cos(angles)
    sinewave = jnp.sin(angles)
    lower_half = values[..., :halfway]
    upper_half = values[..., halfway:]
    return jnp.concatenate(
        [
            lower_half * cosines - upper_half * sinewave,
            upper_half * cosines + lower_half * sinewave,
        ],
        axis=-1,
    )


def attend(queries, key_new, value_new, key_rows, value_rows, length):
    scaling = queries.shape[-1] ** (-0.5)
    scores = (
        jnp.einsum("kgd,kld->kgl", queries, key_rows, preferred_element_type=jnp.float32) * scaling
    )
    visible = jnp.arange(key_rows.shape[1]) < length
    scores = jnp.where(visible, scores, -jnp.inf)
    own_score = (
        jnp.einsum("kgd,kd->kg", queries, key_new, preferred_element_type=jnp.float32) * scaling
    )
    highest = jnp.maximum(jnp.max(scores, axis=-1), own_score)
    shifted = jnp.exp(scores - highest[..., None])
    own_term = jnp.exp(own_score - highest)
    totals = jnp.sum(shifted, axis=-1) + own_term
    weights = (shifted / totals[..., None]).astype(jnp.bfloat16)
    own_weight = (own_term / totals).astype(jnp.bfloat16)
    attended = jnp.einsum("kgl,kld->kgd", weights, value_rows, preferred_element_type=jnp.float32)
    attended = (
        attended
        + own_weight.astype(jnp.float32)[..., None] * value_new.astype(jnp.float32)[:, None, :]
    )
    return attended.astype(jnp.bfloat16)


def enter(axis, n):
    barrier = pltpu.get_barrier_semaphore()
    me = lax.axis_index(axis)
    for step in range(1, n):
        pl.semaphore_signal(
            barrier, inc=1, device_id={axis: lax.rem(me + step, n)}, device_id_type=MESH
        )
    pl.semaphore_wait(barrier, n - 1)
    return me


def send_all(axis, n, source, target, send_sem, recv_sem):
    me = lax.axis_index(axis)
    copies = []
    for step in range(1, n):
        peer = lax.rem(me + step, n)
        copy = pltpu.make_async_remote_copy(
            src_ref=source(peer),
            dst_ref=target,
            send_sem=send_sem.at[step - 1],
            recv_sem=recv_sem.at[step - 1],
            device_id={axis: peer},
            device_id_type=MESH,
        )
        copy.start()
        copies.append(copy)
    return copies


def finish(copies):
    for copy in copies:
        copy.wait()


def total(arrived, n, columns):
    value = arrived[0, :, columns].astype(jnp.float32)
    for index in range(1, n):
        value = value + arrived[index, :, columns].astype(jnp.float32)
    return value


def sum_kernel(axis, n, blocks, out, arrived, send_sem, recv_sem):
    me = enter(axis, n)
    copies = send_all(axis, n, lambda peer: blocks.at[peer], arrived.at[me], send_sem, recv_sem)
    arrived[me] = blocks[me]
    finish(copies)
    out[...] = total(arrived, n, slice(None))


def spread_kernel(axis, n, block, out, send_sem, recv_sem):
    me = enter(axis, n)
    copies = send_all(axis, n, lambda peer: block, out.at[me], send_sem, recv_sem)
    out[me] = block[...]
    finish(copies)


def add_kernel(axis, n, blocks, stream, out, arrived, send_sem, recv_sem, send_two, recv_two):
    me = enter(axis, n)
    copies = send_all(axis, n, lambda peer: blocks.at[peer], arrived.at[me], send_sem, recv_sem)
    arrived[me] = blocks[me]
    finish(copies)
    out[me] = stream[me] + total(arrived, n, slice(None))
    finish(send_all(axis, n, lambda peer: out.at[me], out.at[me], send_two, recv_two))


def hidden_kernel(
    axis, n, blocks, out, arrived, mine, send_sem, recv_sem, send_two, recv_two
):
    me = enter(axis, n)
    copies = send_all(axis, n, lambda peer: blocks.at[peer], arrived.at[me], send_sem, recv_sem)
    arrived[me] = blocks[me]
    finish(copies)
    rows = blocks.shape[1] // 2
    width = blocks.shape[2] - 128
    half = width // 2
    squares = total(arrived, n, slice(width, width + 128))
    squares = squares[:rows, :1] + squares[rows:, :1]
    factor = lax.rsqrt(squares / D + epsilon)
    step = half // 7
    for start in range(0, half, step):
        parts = []
        for base in (0, half):
            sums = total(arrived, n, slice(base + start, base + start + step))
            gate = sums[:rows] * factor
            up = sums[rows:] * factor
            parts.append(gate / (1.0 + jnp.exp(-gate)) * up)
        mine[:, start : start + step] = jnp.concatenate(parts, axis=0).astype(jnp.bfloat16)
    copies = send_all(axis, n, lambda peer: mine, out.at[me], send_two, recv_two)
    out[me] = mine[...]
    finish(copies)


def call(kernel, axis, shape, dtype, scratch, phases, number, *operands):
    n = lax.axis_size(axis)
    whole = pl.BlockSpec(memory_space=pltpu.VMEM)
    return pl.pallas_call(
        functools.partial(kernel, axis, n),
        out_shape=jax.ShapeDtypeStruct(shape, dtype),
        in_specs=[whole] * len(operands),
        out_specs=whole,
        scratch_shapes=scratch + [pltpu.SemaphoreType.DMA((n - 1,))] * (2 * phases),
        compiler_params=pltpu.CompilerParams(
            collective_id=number, has_side_effects=True, vmem_limit_bytes=24 * 2**20
        ),
    )(*operands)


def sum_to_owner(blocks, axis, number):
    scratch = [pltpu.VMEM(blocks.shape, blocks.dtype)]
    return call(sum_kernel, axis, blocks.shape[1:], jnp.float32, scratch, 1, number, blocks)


def spread_matmul(halves, weights):
    owners, both, half = halves.shape
    left = halves[:, : both // 2].reshape(-1, half)
    right = halves[:, both // 2 :].reshape(-1, half)
    return jnp.dot(
        jnp.concatenate([left, right], axis=1), weights, preferred_element_type=jnp.float32
    )


def add_over_wide(stream, terms, number):
    n = lax.axis_size("wide")
    blocks = terms.reshape(n, terms.shape[0] // n, -1)
    return call(
        add_kernel,
        "wide",
        blocks.shape,
        jnp.float32,
        [pltpu.VMEM(blocks.shape, jnp.float32)],
        2,
        number,
        blocks,
        stream.reshape(blocks.shape),
    ).reshape(terms.shape)


def body(
    hidden_in,
    attn_gain,
    w_query,
    w_key,
    w_value,
    w_out,
    ffn_gain,
    w_gate,
    w_up,
    w_down,
    key_cache,
    value_cache,
    cache_len,
):
    head_size = key_cache.shape[-1]
    micro, local_rows, kv_here = key_cache.shape[:3]
    width = hidden_in.shape[2]
    narrow = lax.axis_size("narrow")
    own_rows = micro * local_rows
    rows = narrow * own_rows
    q_here = w_query.shape[1]
    k_here = w_key.shape[1]
    stream = hidden_in.reshape(micro, narrow, local_rows, width)
    stream = stream.transpose(1, 0, 2, 3).reshape(rows, width)
    squares = jnp.sum(stream * stream, axis=-1, keepdims=True)
    normed = (stream * attn_gain).astype(jnp.bfloat16)
    parts = jnp.concatenate(
        [
            jnp.dot(normed, w_query, preferred_element_type=jnp.float32),
            jnp.dot(normed, w_key, preferred_element_type=jnp.float32),
            jnp.dot(normed, w_value, preferred_element_type=jnp.float32),
            jnp.broadcast_to(squares, (rows, 128)),
        ],
        axis=1,
    )
    sums = sum_to_owner(parts.reshape(narrow, own_rows, -1), "narrow", 0)
    factor = lax.rsqrt(sums[:, -1:] / D + epsilon)
    places = cache_len.reshape(own_rows).astype(jnp.float32)[:, None, None]
    query_rows = sums[:, :q_here] * factor
    key_rows_new = sums[:, q_here : q_here + k_here] * factor
    value_rows_new = sums[:, q_here + k_here : q_here + 2 * k_here] * factor
    queries = rotate(query_rows.reshape(own_rows, -1, head_size), places).astype(jnp.bfloat16)
    keys_new = rotate(key_rows_new.reshape(own_rows, kv_here, head_size), places).astype(
        jnp.bfloat16
    )
    values_new = value_rows_new.reshape(own_rows, kv_here, head_size).astype(jnp.bfloat16)
    attended = jax.vmap(attend)(
        queries.reshape(own_rows, kv_here, -1, head_size),
        keys_new,
        values_new,
        key_cache.reshape((own_rows,) + key_cache.shape[2:]),
        value_cache.reshape((own_rows,) + value_cache.shape[2:]),
        cache_len.reshape(own_rows),
    ).reshape(own_rows, -1)
    half = attended.shape[1] // 2
    attended = jnp.concatenate([attended[:, :half], attended[:, half:]], axis=0)
    spread_shape = (narrow,) + attended.shape
    attended = call(
        spread_kernel, "narrow", spread_shape, jnp.bfloat16, [], 1, 1, attended
    )
    out_terms = spread_matmul(attended, w_out)
    middle = add_over_wide(stream, out_terms, 2)
    squares_two = jnp.sum(middle * middle, axis=-1, keepdims=True)
    coarse = lax.reduce_precision(squares_two, 8, 7)
    fine = squares_two - coarse
    normed_two = (middle * ffn_gain).astype(jnp.bfloat16)
    gate_part = jnp.dot(normed_two, w_gate, preferred_element_type=jnp.float32)
    up_part = jnp.dot(normed_two, w_up, preferred_element_type=jnp.float32)
    def beside(part, square):
        part = [part.astype(jnp.bfloat16), jnp.broadcast_to(square, (rows, 128)).astype(jnp.bfloat16)]
        return jnp.concatenate(part, axis=1).reshape(narrow, own_rows, -1)

    blocks = jnp.concatenate([beside(gate_part, coarse), beside(up_part, fine)], axis=1)
    hidden_shape = (narrow, 2 * own_rows, w_gate.shape[1] // 2)
    scratch = [pltpu.VMEM(blocks.shape, jnp.bfloat16), pltpu.VMEM(hidden_shape[1:], jnp.bfloat16)]
    hidden = call(hidden_kernel, "narrow", hidden_shape, jnp.bfloat16, scratch, 2, 3, blocks)
    down_terms = spread_matmul(hidden, w_down)
    result = add_over_wide(middle, down_terms, 4)
    result = result.reshape(narrow, micro, local_rows, width).transpose(1, 0, 2, 3)
    return result.reshape(hidden_in.shape)


def solution(mesh):
    return jax.shard_map(
        body,
        mesh=mesh,
        in_specs=(
            P(None, None, "narrow"),
            P("narrow"),
            P("narrow", "wide"),
            P("narrow", "wide"),
            P("narrow", "wide"),
            P("wide", "narrow"),
            P("narrow"),
            P("narrow", "wide"),
            P("narrow", "wide"),
            P("wide", "narrow"),
            P(None, "narrow", "wide", None, None),
            P(None, "narrow", "wide", None, None),
            P(None, "narrow"),
        ),
        out_specs=P(None, None, "narrow"),
        check_vma=False,
    )
```
